32 devices in a mesh: inst: 4 (over z), circ: 4 (over x, core), ax: 2 (over y).
Axes of the slice: x: 2, y: 2, z: 4, core: 2. Of those that a mesh axis runs over, the one named last changes fastest.
Arguments:
- state_start: float32 [16, 5, 64, 16, 512], P('inst', None, 'ax', None, 'circ'), may hold values from -6 to 6
- forcing: float32 [16, 5, 64, 16, 512], P('inst', None, 'ax', None, 'circ'), may hold values from -6 to 6
- pseudo_step: float32 [64, 16, 512], P('ax', None, 'circ'), may hold values from 0.1 to 0.4
- flux_jacobians: float32 [3, 5, 5], replicated, may hold values from -3 to 3
- interp_weights: float32 [16, 128, 128], P('inst'), may hold values from -0.5 to 0.5
- sector_shift: int32 [16], P('inst'), may hold values from 0 to 3
Outputs:
- state_final: float32 [16, 5, 64, 16, 512], P('inst', None, 'ax', None, 'circ')
- last_residual: float32 [16, 5, 64, 16, 512], P('inst', None, 'ax', None, 'circ')
The draws below stay inside these ranges and needn't reach their ends.
Inputs may be any that keep to these rules, and one draw needn't show every extreme that they name: `sector_shift`: the rotor's sector offset of an instance.
All inputs are finite; a program needn't handle non-finite values.
Results may differ from the reference program's by a relative error of at most 0.0001.
Values sent between devices are 32-bit elements; how exact they have to be, the bound alone decides.
A program may use at most 256 MiB of HBM per device.

```python
import math
import jax
import jax.numpy as jnp
from jax import lax

NI = 16
NV = 5
CA = 32
CR = 16
CT = 128
ITERS = 2
AXL = 64
TAN = 512
N_CIRC = 4


def set_ends(drawn, key, least, largest):
    longest = drawn.shape.index(max(drawn.shape))
    spots = []
    for shift in (0, 1):
        where = [jax.random.randint(jax.random.fold_in(key, axis), (), 0, length) for axis, length in enumerate(drawn.shape)]
        where[longest] = (where[longest] + shift) % drawn.shape[longest]
        spots.append(tuple(where))
    return drawn.at[spots[0]].set(least).at[spots[1]].set(largest)


def level_of(stream_key, shape, split, smallest, largest):
    def one(position, parts):
        draws = jax.random.uniform(jax.random.fold_in(jax.random.fold_in(stream_key, 6), position), (parts,), jnp.float32, smallest / len(split), largest / len(split))
        return jnp.repeat(jnp.exp(draws), shape[position] // parts).reshape((-1,) + (1,) * (len(shape) - position - 1))

    factor_of = one(*split[0])
    for cut in split[1:]:
        factor_of = factor_of * one(*cut)
    return factor_of


def scatter_about(rng, extent, width, most, split=(), kind=jnp.bfloat16):
    loudness = level_of(rng, extent, split, -0.22, 0.18) if split else 1.0
    array = jax.random.normal(rng, extent, jnp.float32) * width * loudness
    return jnp.minimum(jnp.maximum(array, -most), most).astype(kind)


def setup_inputs(seed: int = 0) -> dict:
    seeds = jax.random.split(jax.random.key(seed), 7)
    state_start = scatter_about(seeds[0], (NI, NV, AXL, CR, TAN), 1.0, 6.0, ((0, 4), (2, 2), (4, 4)), jnp.float32)
    forcing = scatter_about(seeds[1], (NI, NV, AXL, CR, TAN), 1.0, 6.0, ((0, 4), (2, 2), (4, 4)), jnp.float32)
    pseudo_step = jnp.clip(jnp.exp(math.log(0.4) - 1.3862944 * jax.random.uniform(seeds[2], (AXL, CR, TAN), jnp.float32) ** level_of(seeds[2], (AXL, CR, TAN), ((0, 2), (2, 4)), -0.2, 0.2)), 0.1, 0.4)
    flux_jacobians = scatter_about(seeds[3], (3, NV, NV), 0.6, 3.0, (), jnp.float32)
    interp_weights = scatter_about(seeds[4], (NI, CT, CT), CT ** -0.5, 0.5, ((0, 4),), jnp.float32)
    sector_shift = set_ends(jax.random.randint(seeds[5], (NI,), 0, N_CIRC), jax.random.fold_in(seeds[5], 1), 0, N_CIRC - 1).astype(jnp.int32)
    return dict(state_start=state_start, forcing=forcing, pseudo_step=pseudo_step, flux_jacobians=flux_jacobians, interp_weights=interp_weights, sector_shift=sector_shift)


FREQUENCY = 0.25
SMOOTHING = 0.25


def spectral_table(count):
    order = jnp.arange(count, dtype=jnp.int32)
    offsets = order[:, None] - order[None, :]
    safe_gap = jnp.where(offsets == 0, 1, offsets)
    parity = (1 - 2 * jnp.mod(offsets, 2)).astype(jnp.float32)
    angles = jnp.pi * safe_gap.astype(jnp.float32) / count
    entries = 0.5 * FREQUENCY * parity * jnp.cos(angles) / jnp.sin(angles)
    return jnp.where(offsets == 0, 0.0, entries).astype(jnp.float32)


def directional(jacobian, field, before, after):
    central = (after - before) * 0.5
    second = after - 2.0 * field + before
    moved = jnp.einsum('vw,iwarc->ivarc', jacobian, central, precision=lax.Precision.HIGHEST)
    return moved - SMOOTHING * second


def reference(state_start, forcing, pseudo_step, flux_jacobians, interp_weights, sector_shift):
    spectral = spectral_table(NI)
    state = state_start
    zero_axial = jnp.zeros_like(state[:, :, :1])
    zero_radial = jnp.zeros_like(state[:, :, :, :1])
    last_residual = state
    for step in range(ITERS):
        rotor_last = state[:, :, CA - 1]
        stator_first = state[:, :, CA]
        rolled_rotor = jax.vmap(lambda values, offset: jnp.roll(values, offset * CT, axis=-1))(rotor_last, sector_shift)
        rolled_stator = jax.vmap(lambda values, offset: jnp.roll(values, -offset * CT, axis=-1))(stator_first, sector_shift)
        ghost_stator = jnp.einsum('ivrkq,itq->ivrkt', rolled_rotor.reshape(NI, NV, CR, N_CIRC, CT), interp_weights,
                                  precision=lax.Precision.HIGHEST).reshape(NI, NV, CR, N_CIRC * CT)
        ghost_rotor = jnp.einsum('ivrkq,iqt->ivrkt', rolled_stator.reshape(NI, NV, CR, N_CIRC, CT), interp_weights,
                                 precision=lax.Precision.HIGHEST).reshape(NI, NV, CR, N_CIRC * CT)
        after_axial = jnp.concatenate([state[:, :, 1:], zero_axial], axis=2).at[:, :, CA - 1].set(ghost_rotor)
        before_axial = jnp.concatenate([zero_axial, state[:, :, :-1]], axis=2).at[:, :, CA].set(ghost_stator)
        after_radial = jnp.concatenate([state[:, :, :, 1:], zero_radial], axis=3)
        before_radial = jnp.concatenate([zero_radial, state[:, :, :, :-1]], axis=3)
        after_tangent = jnp.roll(state, -1, axis=4)
        before_tangent = jnp.roll(state, 1, axis=4)
        flux = directional(flux_jacobians[0], state, before_axial, after_axial)
        flux = flux + directional(flux_jacobians[1], state, before_radial, after_radial)
        flux = flux + directional(flux_jacobians[2], state, before_tangent, after_tangent)
        coupling = jnp.einsum('nm,mvarc->nvarc', spectral, state, precision=lax.Precision.HIGHEST)
        last_residual = flux + coupling - forcing
        state = state - pseudo_step[None, None] * last_residual
    return state, last_residual
```

```python
import functools
import math

import jax
import jax.numpy as jnp
from jax import lax
from jax.experimental import pallas as pl
from jax.experimental.pallas import tpu as pltpu
from jax.sharding import PartitionSpec as P

FREQUENCY = 0.25
SMOOTHING = 0.25
MESH = pl.DeviceIdType.MESH
HIGHEST = lax.Precision.HIGHEST
MOST_CHUNKS = 4


def derivative(values):
    count = len(values)
    half = count // 2
    factors = {
        k: 0.5 * FREQUENCY * (-1) ** k / math.tan(math.pi * k / count) for k in range(1, half)
    }
    low, high = [], []
    for n in range(half):
        gaps = {k: values[(n - k) % count] - values[(n + k) % count] for k in range(1, half)}
        first, second = None, None
        for k in range(1, half):
            one, two = factors[k] * gaps[k], factors[k] * gaps[half - k]
            first = one if first is None else first + one
            second = -two if second is None else second - two
        low.append(first)
        high.append(second)
    return low + high


def kernel(
    sizes,
    start_ref, forcing_ref, step_ref, jac_ref, weights_ref, turn_ref,
    final_ref, residual_ref,
    state, force, drive, all_state, all_drive, back, coupled, coupled_next,
    faces, edges, edges_in,
    z_send, z_recv, z_local, f_send, f_recv, e_send, e_recv, load_sem, out_sem,
):
    parts, cycle, chunks = sizes
    instances, comps, layers, radial, width = drive.shape
    total = all_state.shape[0]
    owned = layers // parts
    depth = owned // chunks
    me = lax.axis_index("inst")
    sector = lax.axis_index("circ")
    row = lax.axis_index("ax")

    def other(offset):
        return lax.rem(me + offset, parts)

    def at_sector(offset):
        return lax.rem(sector + offset, cycle)

    barrier = pltpu.get_barrier_semaphore()
    for p in range(1, parts):
        pl.semaphore_signal(barrier, inc=1, device_id={"inst": other(p)}, device_id_type=MESH)
    for p in range(cycle):
        pl.semaphore_signal(
            barrier, inc=1, device_id={"circ": at_sector(p), "ax": 1 - row}, device_id_type=MESH
        )
    for p in (1, cycle - 1):
        pl.semaphore_signal(barrier, inc=1, device_id={"circ": at_sector(p)}, device_id_type=MESH)
    pl.semaphore_wait(barrier, parts - 1 + cycle + 2)

    def face_copy(turn, p):
        layer = (1 - row) * (layers - 1)
        source = start_ref.at[:, :, layer] if turn == 0 else state.at[:, :, layer + 1]
        return pltpu.make_async_remote_copy(
            src_ref=source, dst_ref=faces.at[turn, p],
            send_sem=f_send.at[turn, p], recv_sem=f_recv.at[turn, p],
            device_id={"circ": at_sector(p), "ax": 1 - row}, device_id_type=MESH,
        )

    def edge_copy(turn, side):
        return pltpu.make_async_remote_copy(
            src_ref=edges.at[turn], dst_ref=edges_in.at[turn, side],
            send_sem=e_send.at[turn, side], recv_sem=e_recv.at[turn, side],
            device_id={"circ": at_sector(1 if side == 0 else cycle - 1)}, device_id_type=MESH,
        )

    def out_ends(phase, k, target):
        source = start_ref if phase == 0 else drive
        there = all_state if phase == 0 else all_drive
        return (
            source.at[:, :, pl.ds(target * owned + k * depth, depth)],
            there.at[pl.ds(me * instances, instances), :, pl.ds(k * depth, depth)],
        )

    def back_ends(phase, k, target):
        source = back if phase == 2 else all_state
        there = coupled if phase == 2 else coupled_next
        return (
            source.at[pl.ds(target * instances, instances), :, pl.ds(k * depth, depth)],
            there.at[:, :, pl.ds(me * owned + k * depth, depth)],
        )

    def moves(phase, k):
        ends = out_ends if phase < 2 else back_ends
        found = []
        for p in range(1, parts):
            source, there = ends(phase, k, other(p))
            found.append(
                pltpu.make_async_remote_copy(
                    src_ref=source, dst_ref=there,
                    send_sem=z_send.at[phase, k, p - 1], recv_sem=z_recv.at[phase, k, p - 1],
                    device_id={"inst": other(p)}, device_id_type=MESH,
                )
            )
        return found

    def kept(phase, k):
        source, there = (out_ends if phase < 2 else back_ends)(phase, k, me)
        return pltpu.make_async_copy(source, there, z_local.at[phase, k])

    def begin(phase, k):
        for copy in moves(phase, k):
            copy.start()
        kept(phase, k).start()

    def arrived(phase, k):
        for copy in moves(phase, k):
            copy.wait_recv()
        kept(phase, k).wait()

    def sent(phase):
        for k in range(chunks):
            for copy in moves(phase, k):
                copy.wait_send()

    lane = lax.broadcasted_iota(jnp.int32, (radial, width), 1)
    line = lax.broadcasted_iota(jnp.int32, (radial, width), 0)

    def exchange(turn):
        for p in range(cycle):
            if turn == 1:
                face_copy(turn, p).start()

        def pack(i, carry):
            n, v = i // comps, i % comps
            packed = jnp.zeros((radial, width), jnp.float32)
            for a in range(layers):
                cells = state[n, v, a + 1]
                packed = jnp.where(lane == a, pltpu.roll(cells, a + 1, 1), packed)
                packed = jnp.where(lane == layers + a, pltpu.roll(cells, layers + a, 1), packed)
            edges[turn, n, v] = packed
            return carry

        lax.fori_loop(0, instances * comps, pack, 0)
        for side in range(2):
            edge_copy(turn, side).start()
        for p in range(cycle):
            face_copy(turn, p).wait_recv()
        for n in range(instances):
            taken = jnp.full((comps, radial, width), turn_ref[n], jnp.int32)
            facing = faces[turn, 0, n]
            for p in range(1, cycle):
                facing = jnp.where(taken == p, faces[turn, p, n], facing)
            ghost = jnp.dot(
                facing.reshape(comps * radial, width), weights_ref[n],
                precision=HIGHEST, preferred_element_type=jnp.float32,
            ).reshape(comps, radial, width)
            empty = jnp.zeros_like(ghost)
            state[n, :, 0] = jnp.where(row == 1, ghost, empty)
            state[n, :, layers + 1] = jnp.where(row == 0, ghost, empty)
        for side in range(2):
            edge_copy(turn, side).wait_recv()

    def flux(turn):
        def one(i, carry):
            n, a = i // layers, i % layers
            rises, curves, cells = [[], [], []], [], []
            for w in range(comps):
                cell = state[n, w, a + 1]
                before, after = state[n, w, a], state[n, w, a + 2]
                down = jnp.where(line == 0, 0.0, pltpu.roll(cell, 1, 0))
                up = jnp.where(line == radial - 1, 0.0, pltpu.roll(cell, radial - 1, 0))
                left = pltpu.roll(edges_in[turn, 0, n, w], lax.rem(width - a, width), 1)
                left = jnp.where(lane == 0, left, pltpu.roll(cell, 1, 1))
                right = pltpu.roll(edges_in[turn, 1, n, w], width - 1 - layers - a, 1)
                right = jnp.where(lane == width - 1, right, pltpu.roll(cell, width - 1, 1))
                rises[0].append(after - before)
                rises[1].append(up - down)
                rises[2].append(right - left)
                around = ((after + before) + (up + down)) + (right + left)
                curves.append(SMOOTHING * (6.0 * cell - around))
            for v in range(comps):
                value = curves[v] - force[n, v, a]
                for d in range(3):
                    for w in range(comps):
                        value = value + jac_ref[(d * comps + v) * comps + w] * rises[d][w]
                drive[n, v, a] = value
            return carry

        lax.fori_loop(0, instances * layers, one, 0)

    def couple(k):
        def one(i, carry):
            v, at = i // depth, k * depth + i % depth
            for top in range(0, radial, 8):
                rows = pl.ds(top, 8)
                found = derivative([all_state[m, v, at, rows] for m in range(total)])
                for m in range(total):
                    back[m, v, at, rows] = found[m]
            return carry

        lax.fori_loop(0, comps * depth, one, 0)

    def couple_next(k):
        def one(i, carry):
            v, at = i // depth, k * depth + i % depth
            for top in range(0, radial, 8):
                rows = pl.ds(top, 8)
                pace = step_ref[me * owned + at, rows]
                found = derivative(
                    [
                        all_state[m, v, at, rows]
                        - pace * (all_drive[m, v, at, rows] + back[m, v, at, rows])
                        for m in range(total)
                    ]
                )
                for m in range(total):
                    all_state[m, v, at, rows] = found[m]
            return carry

        lax.fori_loop(0, comps * depth, one, 0)

    load_state = pltpu.make_async_copy(
        start_ref, state.at[:, :, pl.ds(1, layers)], load_sem.at[0]
    )
    load_force = pltpu.make_async_copy(forcing_ref, force, load_sem.at[1])
    for p in range(cycle):
        face_copy(0, p).start()
    load_state.start()
    load_force.start()
    for k in range(chunks):
        begin(0, k)
    load_state.wait()
    exchange(0)
    load_force.wait()
    flux(0)
    for k in range(chunks):
        begin(1, k)
    for k in range(chunks):
        arrived(0, k)
        couple(k)
        begin(2, k)
    for k in range(chunks):
        arrived(1, k)
        couple_next(k)
        begin(3, k)
    for k in range(chunks):
        arrived(2, k)

    def advance(i, carry):
        n, a = i // layers, i % layers
        pace = step_ref[a]
        for v in range(comps):
            state[n, v, a + 1] = state[n, v, a + 1] - pace * (drive[n, v, a] + coupled[n, v, a])
        return carry

    lax.fori_loop(0, instances * layers, advance, 0)
    sent(1)
    exchange(1)
    flux(1)

    def results(k, j):
        here = pl.ds(j * owned + k * depth, depth)
        return (
            pltpu.make_async_copy(
                coupled.at[:, :, here], final_ref.at[:, :, here], out_sem.at[0, k, j]
            ),
            pltpu.make_async_copy(
                drive.at[:, :, here], residual_ref.at[:, :, here], out_sem.at[1, k, j]
            ),
        )

    for k in range(chunks):
        arrived(3, k)

        def finish(i, carry):
            n, j, at = i // owned_now, (i % owned_now) // depth, i % depth
            a = j * owned + k * depth + at
            pace = step_ref[a]
            for v in range(comps):
                rest = drive[n, v, a] + coupled_next[n, v, a]
                drive[n, v, a] = rest
                coupled[n, v, a] = state[n, v, a + 1] - pace * rest
            return carry

        owned_now = parts * depth
        lax.fori_loop(0, instances * owned_now, finish, 0)
        for j in range(parts):
            for copy in results(k, j):
                copy.start()
    for k in range(chunks):
        for j in range(parts):
            for copy in results(k, j):
                copy.wait()
    for phase in (0, 2, 3):
        sent(phase)
    for turn in range(2):
        for p in range(cycle):
            face_copy(turn, p).wait_send()
        for side in range(2):
            edge_copy(turn, side).wait_send()


def local(state_start, forcing, pseudo_step, flux_jacobians, interp_weights, sector_shift):
    instances, comps, layers, radial, width = state_start.shape
    parts, cycle = lax.axis_size("inst"), lax.axis_size("circ")
    owned = layers // parts
    chunks = math.gcd(owned, MOST_CHUNKS)
    row = lax.axis_index("ax")
    turns = jnp.where(row == 1, sector_shift, jnp.mod(cycle - sector_shift, cycle))
    weights = jnp.where(row == 1, jnp.swapaxes(interp_weights, 1, 2), interp_weights)
    block = (instances, comps, layers, radial, width)
    gathered = (instances * parts, comps, owned, radial, width)
    face = (instances, comps, radial, width)
    f32 = jnp.float32
    dma = pltpu.SemaphoreType.DMA
    vmem = pl.BlockSpec(memory_space=pltpu.VMEM)
    smem = pl.BlockSpec(memory_space=pltpu.SMEM)
    hbm = pl.BlockSpec(memory_space=pl.ANY)
    whole = jax.ShapeDtypeStruct(block, f32)
    return pl.pallas_call(
        functools.partial(kernel, (parts, cycle, chunks)),
        out_shape=(whole, whole),
        in_specs=[hbm, hbm, vmem, smem, vmem, smem],
        out_specs=(hbm, hbm),
        scratch_shapes=[
            pltpu.VMEM((instances, comps, layers + 2, radial, width), f32),
            pltpu.VMEM(block, f32),
            pltpu.VMEM(block, f32),
            pltpu.VMEM(gathered, f32),
            pltpu.VMEM(gathered, f32),
            pltpu.VMEM(gathered, f32),
            pltpu.VMEM(block, f32),
            pltpu.VMEM(block, f32),
            pltpu.VMEM((2, cycle) + face, f32),
            pltpu.VMEM((2,) + face, f32),
            pltpu.VMEM((2, 2) + face, f32),
            dma((4, chunks, parts - 1)),
            dma((4, chunks, parts - 1)),
            dma((4, chunks)),
            dma((2, cycle)),
            dma((2, cycle)),
            dma((2, 2)),
            dma((2, 2)),
            dma((2,)),
            dma((2, chunks, parts)),
        ],
        compiler_params=pltpu.CompilerParams(
            collective_id=0, has_side_effects=True, vmem_limit_bytes=56 * 1024 * 1024
        ),
    )(state_start, forcing, pseudo_step, flux_jacobians.reshape(-1) * 0.5, weights, turns)


def solution(mesh):
    cells = P("inst", None, "ax", None, "circ")
    placed = (cells, cells, P("ax", None, "circ"), P(), P("inst", None, None), P("inst"))
    return jax.shard_map(
        local, mesh=mesh, in_specs=placed, out_specs=(cells, cells), check_vma=False
    )
```

```python
import functools
import math

import jax
import jax.numpy as jnp
from jax import lax
from jax.experimental import pallas as pl
from jax.experimental.pallas import tpu as pltpu
from jax.sharding import PartitionSpec as P

FREQUENCY = 0.25
SMOOTHING = 0.25
MESH = pl.DeviceIdType.MESH
HIGHEST = lax.Precision.HIGHEST
MOST_CHUNKS = 4


def derivative(values):
    count = len(values)
    half = count // 2
    factors = {
        k: 0.5 * FREQUENCY * (-1) ** k / math.tan(math.pi * k / count) for k in range(1, half)
    }
    low, high = [], []
    for n in range(half):
        gaps = {k: values[(n - k) % count] - values[(n + k) % count] for k in range(1, half)}
        first, second = None, None
        for k in range(1, half):
            one, two = factors[k] * gaps[k], factors[k] * gaps[half - k]
            first = one if first is None else first + one
            second = -two if second is None else second - two
        low.append(first)
        high.append(second)
    return low + high


def kernel(
    sizes,
    start_ref, forcing_ref, step_ref, jac_ref, weights_ref, shift_ref,
    coupled, drive,
    state, force, all_state, all_drive, back, coupled_next,
    faces, edges, edges_in,
    z_send, z_recv, z_local, f_send, f_recv, e_send, e_recv, load_sem,
):
    parts, cycle, chunks = sizes
    instances, comps, layers, radial, width = drive.shape
    total = all_state.shape[0]
    owned = layers // parts
    depth = owned // chunks
    me = lax.axis_index("inst")
    sector = lax.axis_index("circ")
    row = lax.axis_index("ax")

    def other(offset):
        return lax.rem(me + offset, parts)

    def at_sector(offset):
        return lax.rem(sector + offset, cycle)

    barrier = pltpu.get_barrier_semaphore()
    for p in range(1, parts):
        pl.semaphore_signal(barrier, inc=1, device_id={"inst": other(p)}, device_id_type=MESH)
    for p in range(cycle):
        pl.semaphore_signal(
            barrier, inc=1, device_id={"circ": at_sector(p), "ax": 1 - row}, device_id_type=MESH
        )
    for p in (1, cycle - 1):
        pl.semaphore_signal(barrier, inc=1, device_id={"circ": at_sector(p)}, device_id_type=MESH)
    pl.semaphore_wait(barrier, parts - 1 + cycle + 2)

    def face_copy(turn, p):
        layer = (1 - row) * (layers - 1)
        source = start_ref.at[:, :, layer] if turn == 0 else state.at[:, :, layer + 1]
        return pltpu.make_async_remote_copy(
            src_ref=source, dst_ref=faces.at[turn, p],
            send_sem=f_send.at[turn, p], recv_sem=f_recv.at[turn, p],
            device_id={"circ": at_sector(p), "ax": 1 - row}, device_id_type=MESH,
        )

    def edge_copy(turn, side):
        return pltpu.make_async_remote_copy(
            src_ref=edges.at[turn], dst_ref=edges_in.at[turn, side],
            send_sem=e_send.at[turn, side], recv_sem=e_recv.at[turn, side],
            device_id={"circ": at_sector(1 if side == 0 else cycle - 1)}, device_id_type=MESH,
        )

    def out_ends(phase, k, target):
        source = start_ref if phase == 0 else drive
        there = all_state if phase == 0 else all_drive
        return (
            source.at[:, :, pl.ds(target * owned + k * depth, depth)],
            there.at[pl.ds(me * instances, instances), :, pl.ds(k * depth, depth)],
        )

    def back_ends(phase, k, target):
        source = back if phase == 2 else all_state
        there = coupled if phase == 2 else coupled_next
        return (
            source.at[pl.ds(target * instances, instances), :, pl.ds(k * depth, depth)],
            there.at[:, :, pl.ds(me * owned + k * depth, depth)],
        )

    def moves(phase, k):
        ends = out_ends if phase < 2 else back_ends
        found = []
        for p in range(1, parts):
            source, there = ends(phase, k, other(p))
            found.append(
                pltpu.make_async_remote_copy(
                    src_ref=source, dst_ref=there,
                    send_sem=z_send.at[phase, k, p - 1], recv_sem=z_recv.at[phase, k, p - 1],
                    device_id={"inst": other(p)}, device_id_type=MESH,
                )
            )
        return found

    def kept(phase, k):
        source, there = (out_ends if phase < 2 else back_ends)(phase, k, me)
        return pltpu.make_async_copy(source, there, z_local.at[phase, k])

    def begin(phase, k):
        for copy in moves(phase, k):
            copy.start()
        kept(phase, k).start()

    def arrived(phase, k):
        for copy in moves(phase, k):
            copy.wait_recv()
        kept(phase, k).wait()

    def sent(phase):
        for k in range(chunks):
            for copy in moves(phase, k):
                copy.wait_send()

    lane = lax.broadcasted_iota(jnp.int32, (radial, width), 1)
    line = lax.broadcasted_iota(jnp.int32, (radial, width), 0)

    def turned(n):
        shift = shift_ref[n]
        return jnp.where(row == 1, shift, lax.rem(cycle - shift, cycle))

    def blend(n):
        weights = weights_ref[n]
        return jnp.where(row == 1, weights.T, weights)

    def exchange(turn):
        for p in range(cycle):
            if turn == 1:
                face_copy(turn, p).start()

        def pack(i, carry):
            n, v = i // comps, i % comps
            packed = jnp.zeros((radial, width), jnp.float32)
            for a in range(layers):
                cells = state[n, v, a + 1]
                packed = jnp.where(lane == a, pltpu.roll(cells, a + 1, 1), packed)
                packed = jnp.where(lane == layers + a, pltpu.roll(cells, layers + a, 1), packed)
            edges[turn, n, v] = packed
            return carry

        lax.fori_loop(0, instances * comps, pack, 0)
        for side in range(2):
            edge_copy(turn, side).start()
        for p in range(cycle):
            face_copy(turn, p).wait_recv()
        for n in range(instances):
            taken = jnp.full((comps, radial, width), turned(n), jnp.int32)
            facing = faces[turn, 0, n]
            for p in range(1, cycle):
                facing = jnp.where(taken == p, faces[turn, p, n], facing)
            ghost = jnp.dot(
                facing.reshape(comps * radial, width), blend(n),
                precision=HIGHEST, preferred_element_type=jnp.float32,
            ).reshape(comps, radial, width)
            empty = jnp.zeros_like(ghost)
            state[n, :, 0] = jnp.where(row == 1, ghost, empty)
            state[n, :, layers + 1] = jnp.where(row == 0, ghost, empty)
        for side in range(2):
            edge_copy(turn, side).wait_recv()

    def flux(turn):
        def one(i, carry):
            n, a = i // layers, i % layers
            rises, curves, cells = [[], [], []], [], []
            for w in range(comps):
                cell = state[n, w, a + 1]
                before, after = state[n, w, a], state[n, w, a + 2]
                down = jnp.where(line == 0, 0.0, pltpu.roll(cell, 1, 0))
                up = jnp.where(line == radial - 1, 0.0, pltpu.roll(cell, radial - 1, 0))
                left = pltpu.roll(edges_in[turn, 0, n, w], lax.rem(width - a, width), 1)
                left = jnp.where(lane == 0, left, pltpu.roll(cell, 1, 1))
                right = pltpu.roll(edges_in[turn, 1, n, w], width - 1 - layers - a, 1)
                right = jnp.where(lane == width - 1, right, pltpu.roll(cell, width - 1, 1))
                rises[0].append(after - before)
                rises[1].append(up - down)
                rises[2].append(right - left)
                around = ((after + before) + (up + down)) + (right + left)
                curves.append(SMOOTHING * (6.0 * cell - around))
            for v in range(comps):
                value = curves[v] - force[n, v, a]
                for d in range(3):
                    for w in range(comps):
                        value = value + (0.5 * jac_ref[d, v, w]) * rises[d][w]
                drive[n, v, a] = value
            return carry

        lax.fori_loop(0, instances * layers, one, 0)

    def couple(k):
        def one(i, carry):
            v, at = i // depth, k * depth + i % depth
            for top in range(0, radial, 8):
                rows = pl.ds(top, 8)
                found = derivative([all_state[m, v, at, rows] for m in range(total)])
                for m in range(total):
                    back[m, v, at, rows] = found[m]
            return carry

        lax.fori_loop(0, comps * depth, one, 0)

    def couple_next(k):
        def one(i, carry):
            v, at = i // depth, k * depth + i % depth
            for top in range(0, radial, 8):
                rows = pl.ds(top, 8)
                pace = step_ref[me * owned + at, rows]
                found = derivative(
                    [
                        all_state[m, v, at, rows]
                        - pace * (all_drive[m, v, at, rows] + back[m, v, at, rows])
                        for m in range(total)
                    ]
                )
                for m in range(total):
                    all_state[m, v, at, rows] = found[m]
            return carry

        lax.fori_loop(0, comps * depth, one, 0)

    load_state = pltpu.make_async_copy(
        start_ref, state.at[:, :, pl.ds(1, layers)], load_sem.at[0]
    )
    load_force = pltpu.make_async_copy(forcing_ref, force, load_sem.at[1])
    for p in range(cycle):
        face_copy(0, p).start()
    load_state.start()
    load_force.start()
    for k in range(chunks):
        begin(0, k)
    load_state.wait()
    exchange(0)
    load_force.wait()
    flux(0)
    for k in range(chunks):
        begin(1, k)
    for k in range(chunks):
        arrived(0, k)
        couple(k)
        begin(2, k)
    for k in range(chunks):
        arrived(1, k)
        couple_next(k)
        begin(3, k)
    for k in range(chunks):
        arrived(2, k)

    def advance(i, carry):
        n, a = i // layers, i % layers
        pace = step_ref[a]
        for v in range(comps):
            state[n, v, a + 1] = state[n, v, a + 1] - pace * (drive[n, v, a] + coupled[n, v, a])
        return carry

    lax.fori_loop(0, instances * layers, advance, 0)
    sent(1)
    exchange(1)
    flux(1)

    for k in range(chunks):
        arrived(3, k)

        def finish(i, carry):
            n, j, at = i // owned_now, (i % owned_now) // depth, i % depth
            a = j * owned + k * depth + at
            pace = step_ref[a]
            for v in range(comps):
                rest = drive[n, v, a] + coupled_next[n, v, a]
                drive[n, v, a] = rest
                coupled[n, v, a] = state[n, v, a + 1] - pace * rest
            return carry

        owned_now = parts * depth
        lax.fori_loop(0, instances * owned_now, finish, 0)
    for phase in (0, 2, 3):
        sent(phase)
    for turn in range(2):
        for p in range(cycle):
            face_copy(turn, p).wait_send()
        for side in range(2):
            edge_copy(turn, side).wait_send()


def local(state_start, forcing, pseudo_step, flux_jacobians, interp_weights, sector_shift):
    instances, comps, layers, radial, width = state_start.shape
    parts, cycle = lax.axis_size("inst"), lax.axis_size("circ")
    owned = layers // parts
    chunks = math.gcd(owned, MOST_CHUNKS)
    block = (instances, comps, layers, radial, width)
    gathered = (instances * parts, comps, owned, radial, width)
    face = (instances, comps, radial, width)
    f32 = jnp.float32
    dma = pltpu.SemaphoreType.DMA
    vmem = pl.BlockSpec(memory_space=pltpu.VMEM)
    smem = pl.BlockSpec(memory_space=pltpu.SMEM)
    hbm = pl.BlockSpec(memory_space=pl.ANY)
    whole = jax.ShapeDtypeStruct(block, f32)
    return pl.pallas_call(
        functools.partial(kernel, (parts, cycle, chunks)),
        out_shape=(pltpu.VMEM(block, f32), pltpu.VMEM(block, f32)),
        in_specs=[hbm, hbm, vmem, smem, vmem, smem],
        out_specs=(vmem, vmem),
        scratch_shapes=[
            pltpu.VMEM((instances, comps, layers + 2, radial, width), f32),
            pltpu.VMEM(block, f32),
            pltpu.VMEM(gathered, f32),
            pltpu.VMEM(gathered, f32),
            pltpu.VMEM(gathered, f32),
            pltpu.VMEM(block, f32),
            pltpu.VMEM((2, cycle) + face, f32),
            pltpu.VMEM((2,) + face, f32),
            pltpu.VMEM((2, 2) + face, f32),
            dma((4, chunks, parts - 1)),
            dma((4, chunks, parts - 1)),
            dma((4, chunks)),
            dma((2, cycle)),
            dma((2, cycle)),
            dma((2, 2)),
            dma((2, 2)),
            dma((2,)),
        ],
        compiler_params=pltpu.CompilerParams(
            collective_id=0, has_side_effects=True, vmem_limit_bytes=42 * 1024 * 1024
        ),
    )(state_start, forcing, pseudo_step, flux_jacobians, interp_weights, sector_shift)


def solution(mesh):
    cells = P("inst", None, "ax", None, "circ")
    placed = (cells, cells, P("ax", None, "circ"), P(), P("inst", None, None), P("inst"))
    return jax.shard_map(
        local, mesh=mesh, in_specs=placed, out_specs=(cells, cells), check_vma=False
    )
```

```python
import functools
import math

import jax
import jax.numpy as jnp
from jax import lax
from jax.experimental import pallas as pl
from jax.experimental.pallas import tpu as pltpu
from jax.sharding import PartitionSpec as P

FREQUENCY = 0.25
SMOOTHING = 0.25
MESH = pl.DeviceIdType.MESH
HIGHEST = lax.Precision.HIGHEST
MOST_CHUNKS = 4


def derivative(values):
    count = len(values)
    half = count // 2
    factors = {
        k: 0.5 * FREQUENCY * (-1) ** k / math.tan(math.pi * k / count) for k in range(1, half)
    }
    low, high = [], []
    for n in range(half):
        gaps = {k: values[(n - k) % count] - values[(n + k) % count] for k in range(1, half)}
        first, second = None, None
        for k in range(1, half):
            one, two = factors[k] * gaps[k], factors[k] * gaps[half - k]
            first = one if first is None else first + one
            second = -two if second is None else second - two
        low.append(first)
        high.append(second)
    return low + high


def kernel(
    sizes,
    start_ref, forcing_ref, step_whole, jac_ref, weights_whole, shift_ref,
    coupled, drive,
    state, force, all_state, all_drive, back, coupled_next,
    faces, edges, edges_in, step_ref, weights_ref,
    z_send, z_recv, z_local, f_send, f_recv, e_send, e_recv, load_sem,
):
    parts, cycle, chunks = sizes
    instances, comps, layers, radial, width = drive.shape
    total = all_state.shape[0]
    owned = layers // parts
    depth = owned // chunks
    me = lax.axis_index("inst")
    sector = lax.axis_index("circ")
    row = lax.axis_index("ax")

    def other(offset):
        return lax.rem(me + offset, parts)

    def at_sector(offset):
        return lax.rem(sector + offset, cycle)

    barrier = pltpu.get_barrier_semaphore()
    for p in range(1, parts):
        pl.semaphore_signal(barrier, inc=1, device_id={"inst": other(p)}, device_id_type=MESH)
    for p in range(cycle):
        pl.semaphore_signal(
            barrier, inc=1, device_id={"circ": at_sector(p), "ax": 1 - row}, device_id_type=MESH
        )
    for p in (1, cycle - 1):
        pl.semaphore_signal(barrier, inc=1, device_id={"circ": at_sector(p)}, device_id_type=MESH)
    pl.semaphore_wait(barrier, parts - 1 + cycle + 2)

    def face_copy(turn, p):
        layer = (1 - row) * (layers - 1)
        source = start_ref.at[:, :, layer] if turn == 0 else state.at[:, :, layer + 1]
        return pltpu.make_async_remote_copy(
            src_ref=source, dst_ref=faces.at[turn, p],
            send_sem=f_send.at[turn, p], recv_sem=f_recv.at[turn, p],
            device_id={"circ": at_sector(p), "ax": 1 - row}, device_id_type=MESH,
        )

    def edge_copy(turn, side):
        return pltpu.make_async_remote_copy(
            src_ref=edges.at[turn], dst_ref=edges_in.at[turn, side],
            send_sem=e_send.at[turn, side], recv_sem=e_recv.at[turn, side],
            device_id={"circ": at_sector(1 if side == 0 else cycle - 1)}, device_id_type=MESH,
        )

    def out_ends(phase, k, target):
        source = start_ref if phase == 0 else drive
        there = all_state if phase == 0 else all_drive
        return (
            source.at[:, :, pl.ds(target * owned + k * depth, depth)],
            there.at[pl.ds(me * instances, instances), :, pl.ds(k * depth, depth)],
        )

    def back_ends(phase, k, target):
        source = back if phase == 2 else all_state
        there = coupled if phase == 2 else coupled_next
        return (
            source.at[pl.ds(target * instances, instances), :, pl.ds(k * depth, depth)],
            there.at[:, :, pl.ds(me * owned + k * depth, depth)],
        )

    def moves(phase, k):
        ends = out_ends if phase < 2 else back_ends
        found = []
        for p in range(1, parts):
            source, there = ends(phase, k, other(p))
            found.append(
                pltpu.make_async_remote_copy(
                    src_ref=source, dst_ref=there,
                    send_sem=z_send.at[phase, k, p - 1], recv_sem=z_recv.at[phase, k, p - 1],
                    device_id={"inst": other(p)}, device_id_type=MESH,
                )
            )
        return found

    def kept(phase, k):
        source, there = (out_ends if phase < 2 else back_ends)(phase, k, me)
        return pltpu.make_async_copy(source, there, z_local.at[phase, k])

    def begin(phase, k):
        for copy in moves(phase, k):
            copy.start()
        kept(phase, k).start()

    def arrived(phase, k):
        for copy in moves(phase, k):
            copy.wait_recv()
        kept(phase, k).wait()

    def sent(phase):
        for k in range(chunks):
            for copy in moves(phase, k):
                copy.wait_send()

    lane = lax.broadcasted_iota(jnp.int32, (radial, width), 1)
    line = lax.broadcasted_iota(jnp.int32, (radial, width), 0)

    def turned(n):
        shift = shift_ref[n]
        return jnp.where(row == 1, shift, lax.rem(cycle - shift, cycle))

    def blend(n):
        weights = weights_ref[n]
        return jnp.where(row == 1, weights.T, weights)

    def exchange(turn):
        for p in range(cycle):
            if turn == 1:
                face_copy(turn, p).start()

        def pack(i, carry):
            n, v = i // comps, i % comps
            packed = jnp.zeros((radial, width), jnp.float32)
            for a in range(layers):
                cells = state[n, v, a + 1]
                packed = jnp.where(lane == a, pltpu.roll(cells, a + 1, 1), packed)
                packed = jnp.where(lane == layers + a, pltpu.roll(cells, layers + a, 1), packed)
            edges[turn, n, v] = packed
            return carry

        lax.fori_loop(0, instances * comps, pack, 0)
        for side in range(2):
            edge_copy(turn, side).start()
        for p in range(cycle):
            face_copy(turn, p).wait_recv()
        for n in range(instances):
            taken = jnp.full((comps, radial, width), turned(n), jnp.int32)
            facing = faces[turn, 0, n]
            for p in range(1, cycle):
                facing = jnp.where(taken == p, faces[turn, p, n], facing)
            ghost = jnp.dot(
                facing.reshape(comps * radial, width), blend(n),
                precision=HIGHEST, preferred_element_type=jnp.float32,
            ).reshape(comps, radial, width)
            empty = jnp.zeros_like(ghost)
            state[n, :, 0] = jnp.where(row == 1, ghost, empty)
            state[n, :, layers + 1] = jnp.where(row == 0, ghost, empty)
        for side in range(2):
            edge_copy(turn, side).wait_recv()

    def flux(turn):
        def one(i, carry):
            n, a = i // layers, i % layers
            rises, curves, cells = [[], [], []], [], []
            for w in range(comps):
                cell = state[n, w, a + 1]
                before, after = state[n, w, a], state[n, w, a + 2]
                down = jnp.where(line == 0, 0.0, pltpu.roll(cell, 1, 0))
                up = jnp.where(line == radial - 1, 0.0, pltpu.roll(cell, radial - 1, 0))
                left = pltpu.roll(edges_in[turn, 0, n, w], lax.rem(width - a, width), 1)
                left = jnp.where(lane == 0, left, pltpu.roll(cell, 1, 1))
                right = pltpu.roll(edges_in[turn, 1, n, w], width - 1 - layers - a, 1)
                right = jnp.where(lane == width - 1, right, pltpu.roll(cell, width - 1, 1))
                rises[0].append(after - before)
                rises[1].append(up - down)
                rises[2].append(right - left)
                around = ((after + before) + (up + down)) + (right + left)
                curves.append(SMOOTHING * (6.0 * cell - around))
            for v in range(comps):
                value = curves[v] - force[n, v, a]
                for d in range(3):
                    for w in range(comps):
                        value = value + (0.5 * jac_ref[d, v, w]) * rises[d][w]
                drive[n, v, a] = value
            return carry

        lax.fori_loop(0, instances * layers, one, 0)

    def couple(k):
        def one(i, carry):
            v, at = i // depth, k * depth + i % depth
            for top in range(0, radial, 8):
                rows = pl.ds(top, 8)
                found = derivative([all_state[m, v, at, rows] for m in range(total)])
                for m in range(total):
                    back[m, v, at, rows] = found[m]
            return carry

        lax.fori_loop(0, comps * depth, one, 0)

    def couple_next(k):
        def one(i, carry):
            v, at = i // depth, k * depth + i % depth
            for top in range(0, radial, 8):
                rows = pl.ds(top, 8)
                pace = step_ref[me * owned + at, rows]
                found = derivative(
                    [
                        all_state[m, v, at, rows]
                        - pace * (all_drive[m, v, at, rows] + back[m, v, at, rows])
                        for m in range(total)
                    ]
                )
                for m in range(total):
                    all_state[m, v, at, rows] = found[m]
            return carry

        lax.fori_loop(0, comps * depth, one, 0)

    load_state = pltpu.make_async_copy(
        start_ref, state.at[:, :, pl.ds(1, layers)], load_sem.at[0]
    )
    load_force = pltpu.make_async_copy(forcing_ref, force, load_sem.at[1])
    load_step = pltpu.make_async_copy(step_whole, step_ref, load_sem.at[2])
    load_weights = pltpu.make_async_copy(weights_whole, weights_ref, load_sem.at[3])
    for p in range(cycle):
        face_copy(0, p).start()
    load_state.start()
    load_weights.start()
    load_step.start()
    load_force.start()
    for k in range(chunks):
        begin(0, k)
    load_state.wait()
    load_weights.wait()
    load_step.wait()
    exchange(0)
    load_force.wait()
    flux(0)
    for k in range(chunks):
        begin(1, k)
    for k in range(chunks):
        arrived(0, k)
        couple(k)
        begin(2, k)
    for k in range(chunks):
        arrived(1, k)
        couple_next(k)
        begin(3, k)
    for k in range(chunks):
        arrived(2, k)

    def advance(i, carry):
        n, a = i // layers, i % layers
        pace = step_ref[a]
        for v in range(comps):
            state[n, v, a + 1] = state[n, v, a + 1] - pace * (drive[n, v, a] + coupled[n, v, a])
        return carry

    lax.fori_loop(0, instances * layers, advance, 0)
    sent(1)
    exchange(1)
    flux(1)

    for k in range(chunks):
        arrived(3, k)

        def finish(i, carry):
            n, j, at = i // owned_now, (i % owned_now) // depth, i % depth
            a = j * owned + k * depth + at
            pace = step_ref[a]
            for v in range(comps):
                rest = drive[n, v, a] + coupled_next[n, v, a]
                drive[n, v, a] = rest
                coupled[n, v, a] = state[n, v, a + 1] - pace * rest
            return carry

        owned_now = parts * depth
        lax.fori_loop(0, instances * owned_now, finish, 0)
    for phase in (0, 2, 3):
        sent(phase)
    for turn in range(2):
        for p in range(cycle):
            face_copy(turn, p).wait_send()
        for side in range(2):
            edge_copy(turn, side).wait_send()


def local(state_start, forcing, pseudo_step, flux_jacobians, interp_weights, sector_shift):
    instances, comps, layers, radial, width = state_start.shape
    parts, cycle = lax.axis_size("inst"), lax.axis_size("circ")
    owned = layers // parts
    chunks = math.gcd(owned, MOST_CHUNKS)
    block = (instances, comps, layers, radial, width)
    gathered = (instances * parts, comps, owned, radial, width)
    face = (instances, comps, radial, width)
    f32 = jnp.float32
    dma = pltpu.SemaphoreType.DMA
    vmem = pl.BlockSpec(memory_space=pltpu.VMEM)
    smem = pl.BlockSpec(memory_space=pltpu.SMEM)
    hbm = pl.BlockSpec(memory_space=pltpu.HBM)
    whole = jax.ShapeDtypeStruct(block, f32)
    return pl.pallas_call(
        functools.partial(kernel, (parts, cycle, chunks)),
        out_shape=(pltpu.VMEM(block, f32), pltpu.VMEM(block, f32)),
        in_specs=[hbm, hbm, hbm, smem, hbm, smem],
        out_specs=(vmem, vmem),
        scratch_shapes=[
            pltpu.VMEM((instances, comps, layers + 2, radial, width), f32),
            pltpu.VMEM(block, f32),
            pltpu.VMEM(gathered, f32),
            pltpu.VMEM(gathered, f32),
            pltpu.VMEM(gathered, f32),
            pltpu.VMEM(block, f32),
            pltpu.VMEM((2, cycle) + face, f32),
            pltpu.VMEM((2,) + face, f32),
            pltpu.VMEM((2, 2) + face, f32),
            pltpu.VMEM(pseudo_step.shape, f32),
            pltpu.VMEM(interp_weights.shape, f32),
            dma((4, chunks, parts - 1)),
            dma((4, chunks, parts - 1)),
            dma((4, chunks)),
            dma((2, cycle)),
            dma((2, cycle)),
            dma((2, 2)),
            dma((2, 2)),
            dma((4,)),
        ],
        compiler_params=pltpu.CompilerParams(
            collective_id=0, has_side_effects=True, vmem_limit_bytes=50 * 1024 * 1024 + 384 * 1024
        ),
    )(state_start, forcing, pseudo_step, flux_jacobians, interp_weights, sector_shift)


def solution(mesh):
    cells = P("inst", None, "ax", None, "circ")
    placed = (cells, cells, P("ax", None, "circ"), P(), P("inst", None, None), P("inst"))
    return jax.shard_map(
        local, mesh=mesh, in_specs=placed, out_specs=(cells, cells), check_vma=False
    )
```
